512 devices in a mesh: seq: 64 (over z, y), head: 8 (over x, core).
Axes of the slice: x: 4, y: 8, z: 8, core: 2. Of those that a mesh axis runs over, the one named last changes fastest.
Arguments:
- queries: float32 [16384, 4096], P('seq', 'head'), may hold values from -6 to 6
- keys: float32 [16384, 4096], P('seq', 'head'), may hold values from -6 to 6
- values: float32 [16384, 4096], P('seq', 'head'), may hold values from -6 to 6
- out_grad: float32 [16384, 4096], P('seq', 'head'), may hold values from -0.00390625 to 0.00390625
Outputs:
- grad_queries: float32 [16384, 4096], P('seq', 'head')
- grad_keys: float32 [16384, 4096], P('seq', 'head')
- grad_values: float32 [16384, 4096], P('seq', 'head')
The draws below stay inside these ranges and needn't reach their ends.
All inputs are finite; a program needn't handle non-finite values.
Results may differ from the reference program's by a relative error of at most 0.00014.
Values sent between devices are 32-bit elements; how exact they have to be, the bound alone decides.
A program may use at most 128 MiB of HBM per device.

```python
import jax
import jax.numpy as jnp
from jax import lax

DK = 128
GROUP = 256
TOK_DEV = 256
HEADS = 32
TOKENS = 16384


def level_of(own_key, dims, cuts, low, largest):
    loudness, own = 1.0, jax.random.fold_in(own_key, 6)
    for position, blocks in cuts:
        heights = jnp.exp(jax.random.uniform(jax.random.fold_in(own, position), (blocks,), jnp.float32, low / len(cuts), largest / len(cuts)))
        loudness = loudness * jnp.repeat(heights, dims[position] // blocks).reshape([-1 if axis == position else 1 for axis in range(len(dims))])
    return loudness


def scatter_about(key, shape, width, bound, pieces=(), dtype=jnp.bfloat16):
    level = level_of(key, shape, pieces, -0.22, 0.18) if pieces else 1.0
    drawn = jax.random.normal(key, shape, jnp.float32) * width * level
    return jnp.minimum(jnp.maximum(drawn, -bound), bound).astype(dtype)


def setup_inputs(seed: int = 0) -> dict:
    key_of = jax.random.split(jax.random.key(seed), 5)
    queries = scatter_about(key_of[0], (TOKENS, HEADS * DK), 1.0, 6.0, ((0, 64), (1, 8)), jnp.float32)
    keys = scatter_about(key_of[1], (TOKENS, HEADS * DK), 1.0, 6.0, ((0, 64), (1, 8)), jnp.float32)
    values = scatter_about(key_of[2], (TOKENS, HEADS * DK), 1.0, 6.0, ((0, 64), (1, 8)), jnp.float32)
    out_grad = scatter_about(key_of[3], (TOKENS, HEADS * DK), (DK * TOKENS) ** -0.5, 0.00390625, ((0, 64), (1, 8)), jnp.float32)
    return {"queries": queries, "keys": keys, "values": values, "out_grad": out_grad}


def reference(queries, keys, values, out_grad):
    hi = lax.Precision.HIGHEST
    block = min(GROUP, TOK_DEV)
    count = TOKENS // block
    shape = (count, block, HEADS, DK)
    q_all = queries.reshape(shape)
    k_all = keys.reshape(shape)
    v_all = values.reshape(shape)
    g_all = out_grad.reshape(shape)
    rows = lax.broadcasted_iota(jnp.int32, (block, block), 0)
    cols = lax.broadcasted_iota(jnp.int32, (block, block), 1)
    causal = (rows >= cols).astype(jnp.float32)

    def forward(state, items):
        q_blk, k_blk, v_blk, g_blk = items
        dscores = jnp.einsum('thd,shd->hts', g_blk, v_blk, precision=hi) * causal
        grad_q = jnp.einsum('hts,shd->thd', dscores, k_blk, precision=hi)
        grad_q = grad_q + jnp.einsum('the,hde->thd', g_blk, state, precision=hi)
        state = state + jnp.einsum('shd,she->hde', k_blk, v_blk, precision=hi)
        return state, grad_q

    def backward(state, items):
        q_blk, k_blk, v_blk, g_blk = items
        scores = jnp.einsum('thd,shd->hts', q_blk, k_blk, precision=hi) * causal
        dscores = jnp.einsum('thd,shd->hts', g_blk, v_blk, precision=hi) * causal
        grad_k = jnp.einsum('hts,thd->shd', dscores, q_blk, precision=hi)
        grad_k = grad_k + jnp.einsum('she,hde->shd', v_blk, state, precision=hi)
        grad_v = jnp.einsum('hts,the->she', scores, g_blk, precision=hi)
        grad_v = grad_v + jnp.einsum('shd,hde->she', k_blk, state, precision=hi)
        state = state + jnp.einsum('thd,the->hde', q_blk, g_blk, precision=hi)
        return state, (grad_k, grad_v)

    start = jnp.zeros((HEADS, DK, DK), jnp.float32)
    items = (q_all, k_all, v_all, g_all)
    _, grad_q = lax.scan(forward, start, items)
    _, (grad_k, grad_v) = lax.scan(backward, start, items, reverse=True)
    flat = (TOKENS, HEADS * DK)
    return grad_q.reshape(flat), grad_k.reshape(flat), grad_v.reshape(flat)
```

```python
import functools

import jax
import jax.numpy as jnp
from jax import lax
from jax.experimental import pallas as pl
from jax.experimental.pallas import tpu as pltpu
from jax.sharding import PartitionSpec as P

DK = 128
RING = 8
MESH = pl.DeviceIdType.MESH
F32 = jnp.float32
BF16 = jnp.bfloat16
OFFSETS = (4, 3, 5, 2, 6, 1, 7)

NT = (((1,), (1,)), ((), ()))
NN = (((1,), (0,)), ((), ()))


def split(x):
    hi = x.astype(BF16)
    lo = (x - hi.astype(F32)).astype(BF16)
    return hi, lo


def left(x, axis):
    hi, lo = split(x)
    return jnp.concatenate([hi, lo, hi], axis=axis)


def right(x, axis):
    hi, lo = split(x)
    return jnp.concatenate([hi, hi, lo], axis=axis)


def product(a, b, dims):
    (ca,), (cb,) = dims[0]
    return lax.dot_general(left(a, ca), right(b, cb), dims, preferred_element_type=F32)


def kernel(heads, q_hbm, k_hbm, v_hbm, g_hbm, oq_hbm, ok_hbm, ov_hbm,
           q_v, k_v, v_v, g_v, aq, ak, av, local, row_in, row_out, total, col_in, back,
           load_sem, store_sem, send_sem, row_sem, col_sem, back_sem):
    me = lax.axis_index("seq")
    hd = lax.axis_index("head")
    z = lax.div(me, RING)
    y = lax.rem(me, RING)
    length = q_v.shape[1]
    part = DK // RING

    def in_row(d):
        return lax.rem(y + d, RING)

    def row_peer(d):
        return (z * RING + in_row(d), hd)

    def col_peer(d):
        return (lax.rem(z + d, RING) * RING + y, hd)

    barrier = pltpu.get_barrier_semaphore()
    for d in OFFSETS:
        pl.semaphore_signal(barrier, inc=1, device_id=row_peer(d), device_id_type=MESH)
        pl.semaphore_signal(barrier, inc=1, device_id=col_peer(d), device_id_type=MESH)

    def columns(h):
        return pl.ds(h * DK, DK)

    def load(i, h):
        hbm, vmem = ((k_hbm, k_v), (v_hbm, v_v), (q_hbm, q_v), (g_hbm, g_v))[i]
        return pltpu.make_async_copy(hbm.at[:, columns(h)], vmem.at[h], load_sem.at[i, h])

    for h in range(heads):
        for i in range(4):
            load(i, h).start()

    def send_row(h, d):
        return pltpu.make_async_remote_copy(
            src_ref=local.at[h, in_row(d)], dst_ref=row_in.at[h, y],
            send_sem=send_sem.at[0, h], recv_sem=row_sem.at[h], device_id=row_peer(d), device_id_type=MESH)

    def send_col(h, d):
        wrapped = lax.div(z + d, RING)
        return pltpu.make_async_remote_copy(
            src_ref=total.at[h, wrapped], dst_ref=col_in.at[h, d - 1],
            send_sem=send_sem.at[1, h], recv_sem=col_sem.at[h], device_id=col_peer(d), device_id_type=MESH)

    def send_back(h, d):
        return pltpu.make_async_remote_copy(
            src_ref=row_out.at[h, in_row(d)], dst_ref=back.at[h, y],
            send_sem=send_sem.at[2, h], recv_sem=back_sem.at[h], device_id=row_peer(d), device_id_type=MESH)

    def all_of(ref, count, sem):
        pltpu.make_async_copy(ref.at[pl.ds(0, count)], ref.at[pl.ds(0, count)], sem).wait()

    for h in range(heads):
        load(0, h).wait()
        load(1, h).wait()
        local[h, :, 0] = product(k_v[h].T, v_v[h], NN).reshape(RING, part, DK)
        load(2, h).wait()
        load(3, h).wait()
        local[h, :, 1] = product(q_v[h].T, g_v[h], NN).reshape(RING, part, DK)
        if h == 0:
            pl.semaphore_wait(barrier, 2 * (RING - 1))
        for d in OFFSETS:
            send_row(h, d).start()
        row_in[h, y] = local[h, y]

    rows = lax.broadcasted_iota(jnp.int32, (length, length), 0)
    cols = lax.broadcasted_iota(jnp.int32, (length, length), 1)
    for h in range(heads):
        q, k, v, g = q_v[h], k_v[h], v_v[h], g_v[h]
        scores_t = jnp.where(rows <= cols, product(k, q, NT), 0.0)
        av[h] = product(scores_t, g, NN)
        dscores = jnp.where(rows >= cols, product(g, v, NT), 0.0)
        aq[h] = product(dscores, k, NN)
        dscores_t = jnp.where(rows <= cols, product(v, g, NT), 0.0)
        ak[h] = product(dscores_t, q, NN)

    def row_step(h):
        all_of(row_in.at[h], RING - 1, row_sem.at[h])
        run = jnp.zeros((part, DK), F32)
        for j in range(RING):
            row_out[h, j, 0] = run
            run = run + row_in[h, j, 0]
        total[h, 0] = run
        run = jnp.zeros((part, DK), F32)
        for j in reversed(range(RING)):
            row_out[h, j, 1] = run
            run = run + row_in[h, j, 1]
        total[h, 1] = run
        for d in OFFSETS:
            send_col(h, d).start()

    def col_step(h):
        all_of(col_in.at[h], RING - 1, col_sem.at[h])
        earlier = jnp.zeros((part, DK), F32)
        later = jnp.zeros((part, DK), F32)
        for d in range(1, RING):
            came = col_in[h, d - 1]
            smaller = z >= d
            earlier = earlier + jnp.where(smaller, came, 0.0)
            later = later + jnp.where(smaller, 0.0, came)
        for j in range(RING):
            row_out[h, j, 0] = row_out[h, j, 0] + earlier
            row_out[h, j, 1] = row_out[h, j, 1] + later
        for d in OFFSETS:
            send_back(h, d).start()
        back[h, y] = row_out[h, y]

    def store(i, h):
        acc, hbm = ((aq, oq_hbm), (ak, ok_hbm), (av, ov_hbm))[i]
        return pltpu.make_async_copy(acc.at[h], hbm.at[:, columns(h)], store_sem.at[i, h])

    def last_step(h):
        all_of(back.at[h], RING - 1, back_sem.at[h])
        prefix = back[h, :, 0].reshape(DK, DK)
        suffix = back[h, :, 1].reshape(DK, DK)
        aq[h] = aq[h] + product(g_v[h], prefix, NT)
        store(0, h).start()
        ak[h] = ak[h] + product(v_v[h], suffix, NT)
        store(1, h).start()
        av[h] = av[h] + product(k_v[h], suffix, NN)
        store(2, h).start()

    lag = 2
    for step in range(heads + lag):
        if step < heads:
            row_step(step)
        if step >= lag:
            col_step(step - lag)
    for h in range(heads):
        last_step(h)
    for h in range(heads):
        for i in range(3):
            store(i, h).wait()
        all_of(local.at[h], RING - 1, send_sem.at[0, h])
        all_of(col_in.at[h], RING - 1, send_sem.at[1, h])
        all_of(row_out.at[h], RING - 1, send_sem.at[2, h])


def shards(queries, keys, values, out_grad):
    length, width = queries.shape
    heads = width // DK
    part = DK // RING
    out = jax.ShapeDtypeStruct((length, width), F32)
    block = pltpu.VMEM((heads, length, DK), F32)
    pieces = pltpu.VMEM((heads, RING, 2, part, DK), F32)
    return pl.pallas_call(
        functools.partial(kernel, heads),
        out_shape=(out, out, out),
        in_specs=[pl.BlockSpec(memory_space=pl.ANY)] * 4,
        out_specs=(pl.BlockSpec(memory_space=pl.ANY),) * 3,
        scratch_shapes=[block] * 7 + [
            pieces,
            pieces,
            pieces,
            pltpu.VMEM((heads, 2, part, DK), F32),
            pltpu.VMEM((heads, RING - 1, part, DK), F32),
            pieces,
            pltpu.SemaphoreType.DMA((4, heads)),
            pltpu.SemaphoreType.DMA((3, heads)),
            pltpu.SemaphoreType.DMA((3, heads)),
            pltpu.SemaphoreType.DMA((heads,)),
            pltpu.SemaphoreType.DMA((heads,)),
            pltpu.SemaphoreType.DMA((heads,)),
        ],
        compiler_params=pltpu.CompilerParams(
            collective_id=0, has_side_effects=True, vmem_limit_bytes=32 * 2**20),
        cost_estimate=pl.CostEstimate(
            flops=2 * 3 * heads * length * DK * (6 * length + 5 * DK),
            bytes_accessed=7 * 4 * length * width, transcendentals=0),
        name="linear_attention_backward",
    )(queries, keys, values, out_grad)


def solution(mesh):
    return jax.shard_map(
        shards,
        mesh=mesh,
        in_specs=(P("seq", "head"),) * 4,
        out_specs=(P("seq", "head"),) * 3,
        check_vma=False,
    )
```

```python
import functools

import jax
import jax.numpy as jnp
from jax import lax
from jax.experimental import pallas as pl
from jax.experimental.pallas import tpu as pltpu
from jax.sharding import PartitionSpec as P

DK = 128
RING = 8
MESH = pl.DeviceIdType.MESH
F32 = jnp.float32
BF16 = jnp.bfloat16
OFFSETS = (4, 3, 5, 2, 6, 1, 7)
PER = 2

NT = (((1,), (1,)), ((), ()))
NN = (((1,), (0,)), ((), ()))


def split(x):
    hi = x.astype(BF16)
    lo = (x - hi.astype(F32)).astype(BF16)
    return hi, lo


def left(x, axis):
    hi, lo = split(x)
    return jnp.concatenate([hi, lo, hi], axis=axis)


def right(x, axis):
    hi, lo = split(x)
    return jnp.concatenate([hi, hi, lo], axis=axis)


def product(a, b, dims):
    (ca,), (cb,) = dims[0]
    return lax.dot_general(left(a, ca), right(b, cb), dims, preferred_element_type=F32)


def kernel(heads, q_hbm, k_hbm, v_hbm, g_hbm, aq, ak, av,
           q_v, k_v, v_v, g_v, local, row_in, row_out, total, col_in, back,
           load_sem, row_send, row_sem, col_send, col_sem, back_send, back_sem, ready):
    me = lax.axis_index("seq")
    hd = lax.axis_index("head")
    z = lax.div(me, RING)
    y = lax.rem(me, RING)
    length = q_v.shape[1]
    part = DK // RING
    chunks = heads // PER

    def in_row(d):
        return lax.rem(y + d, RING)

    def row_peer(d):
        return (z * RING + in_row(d), hd)

    def in_column(other):
        return (other * RING + y, hd)

    barrier = pltpu.get_barrier_semaphore()
    for d in OFFSETS:
        pl.semaphore_signal(barrier, inc=1, device_id=row_peer(d), device_id_type=MESH)

    def greet(d, _):
        pl.semaphore_signal(barrier, inc=1, device_id=in_column(z + d), device_id_type=MESH)
        return _

    lax.fori_loop(1, RING - z, greet, 0)

    def columns(h):
        return pl.ds(h * DK, DK)

    def load(i, h):
        hbm, vmem = ((k_hbm, k_v), (v_hbm, v_v), (q_hbm, q_v), (g_hbm, g_v))[i]
        return pltpu.make_async_copy(hbm.at[:, columns(h)], vmem.at[h], load_sem.at[i, h])

    def send_row(t, h, d):
        return pltpu.make_async_remote_copy(
            src_ref=local.at[t, h, in_row(d)], dst_ref=row_in.at[t, h, y],
            send_sem=row_send.at[t, h], recv_sem=row_sem.at[t, h], device_id=row_peer(d), device_id_type=MESH)

    def send_col(t, h, d):
        return pltpu.make_async_remote_copy(
            src_ref=total.at[t, h], dst_ref=col_in.at[t, h, d - 1],
            send_sem=col_send.at[t, h, d - 1], recv_sem=col_sem.at[t, h, d - 1],
            device_id=in_column(z - d if t else z + d), device_id_type=MESH)

    def send_back(t, h, d):
        return pltpu.make_async_remote_copy(
            src_ref=row_out.at[t, h, in_row(d)], dst_ref=back.at[t, h, y],
            send_sem=back_send.at[t, h], recv_sem=back_sem.at[t, h], device_id=row_peer(d), device_id_type=MESH)

    def all_of(ref, sem):
        some = ref.at[pl.ds(0, RING - 1)]
        pltpu.make_async_copy(some, some, sem).wait()

    def larger(t):
        return (z, RING - 1 - z) if t else (RING - 1 - z, z)

    def state(t, c):
        a, b = (q_v, g_v) if t else (k_v, v_v)
        for i in range(PER):
            h = c * PER + i
            load(2 * t, h).wait()
            load(2 * t + 1, h).wait()
            local[t, c, :, pl.ds(i * part, part)] = product(a[h].T, b[h], NN).reshape(RING, part, DK)

    def row_start(t, h):
        for d in OFFSETS:
            send_row(t, h, d).start()
        row_in[t, h, y] = local[t, h, y]

    def within(h):
        rows = lax.broadcasted_iota(jnp.int32, (length, length), 0)
        cols = lax.broadcasted_iota(jnp.int32, (length, length), 1)
        q, k, v, g = q_v[h], k_v[h], v_v[h], g_v[h]
        scores_t = jnp.where(rows <= cols, product(k, q, NT), 0.0)
        av[:, columns(h)] = product(scores_t, g, NN)
        dscores = jnp.where(rows >= cols, product(g, v, NT), 0.0)
        aq[:, columns(h)] = product(dscores, k, NN)
        dscores_t = jnp.where(rows <= cols, product(v, g, NT), 0.0)
        ak[:, columns(h)] = product(dscores_t, q, NN)

    def row_step(t, h):
        all_of(row_in.at[t, h], row_sem.at[t, h])
        run = jnp.zeros((PER * part, DK), F32)
        for j in (reversed(range(RING)) if t else range(RING)):
            row_out[t, h, j] = run
            run = run + row_in[t, h, j]
        total[t, h] = run
        if t == 0 and h == 0:

            @pl.when(z < RING - 1)
            def _():
                pl.semaphore_wait(ready, RING - 1 - z)

        count = larger(t)[0]

        def send(i, _):
            send_col(t, h, count - i).start()
            return _

        lax.fori_loop(0, count, send, 0)

    def col_step(t, h):
        def add(i, beyond):
            send_col(t, h, i + 1).wait_recv()
            return beyond + col_in[t, h, i]

        beyond = lax.fori_loop(0, larger(t)[1], add, jnp.zeros((PER * part, DK), F32))
        for j in range(RING):
            row_out[t, h, j] = row_out[t, h, j] + beyond
        for d in OFFSETS:
            send_back(t, h, d).start()
        back[t, h, y] = row_out[t, h, y]

    def last_step(t, c):
        all_of(back.at[t, c], back_sem.at[t, c])
        for i in range(PER):
            h = c * PER + i
            state = back[t, c, :, pl.ds(i * part, part)].reshape(DK, DK)
            if t:
                ak[:, columns(h)] = ak[:, columns(h)] + product(v_v[h], state, NT)
                av[:, columns(h)] = av[:, columns(h)] + product(k_v[h], state, NN)
            else:
                aq[:, columns(h)] = aq[:, columns(h)] + product(g_v[h], state, NT)

    def work(kinds, ahead, lag):
        order = [(t, c) for t in kinds for c in range(chunks)]
        for t in kinds:
            for h in range(heads):
                load(2 * t, h).start()
                load(2 * t + 1, h).start()
        for n, (t, c) in enumerate(order):
            state(t, c)
            if n == 0:
                pl.semaphore_wait(barrier, RING - 1 + z)

                def tell(d, _):
                    pl.semaphore_signal(ready, inc=1, device_id=in_column(z - d), device_id_type=MESH)
                    return _

                lax.fori_loop(1, z + 1, tell, 0)
            if n < ahead:
                row_start(t, c)
        for step in range(len(order) + lag):
            if step < chunks:
                for i in range(PER):
                    within(step * PER + i)
            if step < len(order):
                row_step(*order[step])
            if step + ahead < len(order):
                row_start(*order[step + ahead])
            if step >= lag:
                col_step(*order[step - lag])
        for t, c in order:
            last_step(t, c)

    @pl.when(z < RING // 2)
    def _():
        work((0, 1), 4, 2)

    @pl.when(z >= RING // 2)
    def _():
        work((1, 0), 4, 2)

    for t in range(2):
        for h in range(chunks):
            all_of(local.at[t, h], row_send.at[t, h])
            all_of(row_out.at[t, h], back_send.at[t, h])

            def sent(i, _):
                send_col(t, h, i + 1).wait_send()
                return _

            lax.fori_loop(0, larger(t)[0], sent, 0)


def write_out(aq, ak, av, oq, ok, ov, sem):
    slabs = sem.shape[1]
    rows = aq.shape[0] // slabs
    copies = []
    for i, (a, o) in enumerate(((aq, oq), (ak, ok), (av, ov))):
        for j in range(slabs):
            here = pl.ds(j * rows, rows)
            copies.append(pltpu.make_async_copy(a.at[here], o.at[here], sem.at[i, j]))
    for copy in copies:
        copy.start()
    for copy in copies:
        copy.wait()


def shards(queries, keys, values, out_grad):
    length, width = queries.shape
    heads = width // DK
    part = DK // RING
    chunks = heads // PER
    held = pltpu.VMEM((length, width), F32)
    out = pltpu.HBM((length, width), F32)
    arrays = [pltpu.with_memory_space_constraint(a, pltpu.HBM) for a in (queries, keys, values, out_grad)]
    block = pltpu.VMEM((heads, length, DK), F32)
    pieces = pltpu.VMEM((2, chunks, RING, PER * part, DK), F32)
    grads = pl.pallas_call(
        functools.partial(kernel, heads),
        out_shape=(held, held, held),
        in_specs=[pl.BlockSpec(memory_space=pltpu.HBM)] * 4,
        out_specs=(pl.BlockSpec(memory_space=pltpu.VMEM),) * 3,
        scratch_shapes=[block] * 4 + [
            pieces,
            pieces,
            pieces,
            pltpu.VMEM((2, chunks, PER * part, DK), F32),
            pltpu.VMEM((2, chunks, RING - 1, PER * part, DK), F32),
            pieces,
            pltpu.SemaphoreType.DMA((4, heads)),
            pltpu.SemaphoreType.DMA((2, chunks)),
            pltpu.SemaphoreType.DMA((2, chunks)),
            pltpu.SemaphoreType.DMA((2, chunks, RING - 1)),
            pltpu.SemaphoreType.DMA((2, chunks, RING - 1)),
            pltpu.SemaphoreType.DMA((2, chunks)),
            pltpu.SemaphoreType.DMA((2, chunks)),
            pltpu.SemaphoreType.REGULAR,
        ],
        compiler_params=pltpu.CompilerParams(
            collective_id=0, has_side_effects=True, vmem_limit_bytes=32 * 2**20),
        cost_estimate=pl.CostEstimate(
            flops=2 * 3 * heads * length * DK * (6 * length + 5 * DK),
            bytes_accessed=7 * 4 * length * width, transcendentals=0),
        name="linear_attention_backward",
    )(*arrays)
    return pl.pallas_call(
        write_out,
        out_shape=(out, out, out),
        in_specs=[pl.BlockSpec(memory_space=pltpu.VMEM)] * 3,
        out_specs=(pl.BlockSpec(memory_space=pltpu.HBM),) * 3,
        scratch_shapes=[pltpu.SemaphoreType.DMA((3, 4))],
        name="write_out",
    )(*[pltpu.with_memory_space_constraint(a, pltpu.VMEM) for a in grads])


def solution(mesh):
    return jax.shard_map(
        shards,
        mesh=mesh,
        in_specs=(P("seq", "head"),) * 4,
        out_specs=(P("seq", "head"),) * 3,
        check_vma=False,
    )
```

```python
import functools

import jax
import jax.numpy as jnp
from jax import lax
from jax.experimental import pallas as pl
from jax.experimental.pallas import tpu as pltpu
from jax.sharding import PartitionSpec as P

DK = 128
RING = 8
MESH = pl.DeviceIdType.MESH
F32 = jnp.float32
BF16 = jnp.bfloat16
OFFSETS = (4, 3, 2, 1, 5, 6, 7)
PER = 2

NT = (((1,), (1,)), ((), ()))
NN = (((1,), (0,)), ((), ()))


def split(x):
    hi = x.astype(BF16)
    lo = (x - hi.astype(F32)).astype(BF16)
    return hi, lo


def left(x, axis):
    hi, lo = split(x)
    return jnp.concatenate([hi, lo, hi], axis=axis)


def right(x, axis):
    hi, lo = split(x)
    return jnp.concatenate([hi, hi, lo], axis=axis)


def dot(a, b, dims):
    return lax.dot_general(a, b, dims, preferred_element_type=F32)


def product(a, b, dims):
    (ca,), (cb,) = dims[0]
    return dot(left(a, ca), right(b, cb), dims)


def kernel(heads, q_hbm, k_hbm, v_hbm, g_hbm, aq, ak, av,
           q_v, k_v, v_v, g_v, parts, local, row_in, row_out, total, col_in, back,
           load_sem, row_send, row_sem, col_send, col_sem, back_send, back_sem, ready):
    me = lax.axis_index("seq")
    hd = lax.axis_index("head")
    z = lax.div(me, RING)
    y = lax.rem(me, RING)
    length = q_v.shape[1]
    part = DK // RING
    chunks = heads // PER

    def in_row(d):
        return lax.rem(y + jnp.where(lax.rem(hd, 2) == 0, d, RING - d), RING)

    def row_peer(d):
        return (z * RING + in_row(d), hd)

    def in_column(other):
        return (other * RING + y, hd)

    barrier = pltpu.get_barrier_semaphore()
    for d in OFFSETS:
        pl.semaphore_signal(barrier, inc=1, device_id=row_peer(d), device_id_type=MESH)

    def greet_column():
        def greet(d, _):
            pl.semaphore_signal(barrier, inc=1, device_id=in_column(z + d), device_id_type=MESH)
            return _

        lax.fori_loop(1, RING - z, greet, 0)

    def meet():
        pl.semaphore_wait(barrier, RING - 1 + z)

        def tell(d, _):
            pl.semaphore_signal(ready, inc=1, device_id=in_column(z - d), device_id_type=MESH)
            return _

        lax.fori_loop(1, z + 1, tell, 0)

    def columns(h):
        return pl.ds(h * DK, DK)

    def load(i, h):
        hbm, vmem = ((k_hbm, k_v), (v_hbm, v_v), (q_hbm, q_v), (g_hbm, g_v))[i]
        return pltpu.make_async_copy(hbm.at[:, columns(h)], vmem.at[h], load_sem.at[i, h])

    def send_row(t, c, d, first, count):
        some = pl.ds(first * part, count * part)
        return pltpu.make_async_remote_copy(
            src_ref=local.at[t, c, in_row(d), some], dst_ref=row_in.at[t, c, y, some],
            send_sem=row_send.at[t, c], recv_sem=row_sem.at[t, c], device_id=row_peer(d), device_id_type=MESH)

    def send_col(t, h, d):
        return pltpu.make_async_remote_copy(
            src_ref=total.at[t, h], dst_ref=col_in.at[t, h, d - 1],
            send_sem=col_send.at[t, h, d - 1], recv_sem=col_sem.at[t, h, d - 1],
            device_id=in_column(z - d if t else z + d), device_id_type=MESH)

    def send_back(t, h, d):
        return pltpu.make_async_remote_copy(
            src_ref=row_out.at[t, h, in_row(d)], dst_ref=back.at[t, h, y],
            send_sem=back_send.at[t, h], recv_sem=back_sem.at[t, h], device_id=row_peer(d), device_id_type=MESH)

    def all_of(ref, sem):
        some = ref.at[pl.ds(0, RING - 1)]
        pltpu.make_async_copy(some, some, sem).wait()

    def larger(t):
        return (z, RING - 1 - z) if t else (RING - 1 - z, z)

    def state(t, c, i):
        a, b = (q_v, g_v) if t else (k_v, v_v)
        h = c * PER + i
        load(2 * t, h).wait()
        load(2 * t + 1, h).wait()
        local[t, c, :, pl.ds(i * part, part)] = product(a[h].T, b[h], NN).reshape(RING, part, DK)

    def row_start(t, c, first, count):
        for d in OFFSETS:
            send_row(t, c, d, first, count).start()

    def within(h):
        rows = lax.broadcasted_iota(jnp.int32, (length, length), 0)
        cols = lax.broadcasted_iota(jnp.int32, (length, length), 1)
        q, k, v, g = q_v[h], k_v[h], v_v[h], g_v[h]
        k_left, v_left, g_left = left(k, 1), left(v, 1), left(g, 1)
        parts[0, h] = k_left
        parts[1, h] = v_left
        parts[2, h] = g_left
        scores_t = jnp.where(rows <= cols, dot(k_left, right(q, 1), NT), 0.0)
        av[:, columns(h)] = product(scores_t, g, NN)
        dscores = jnp.where(rows >= cols, dot(g_left, right(v, 1), NT), 0.0)
        aq[:, columns(h)] = product(dscores, k, NN)
        dscores_t = jnp.where(rows <= cols, dot(v_left, right(g, 1), NT), 0.0)
        ak[:, columns(h)] = product(dscores_t, q, NN)

    def row_step(t, h):
        all_of(row_in.at[t, h], row_sem.at[t, h])
        run = jnp.zeros((PER * part, DK), F32)
        for j in (reversed(range(RING)) if t else range(RING)):
            row_out[t, h, j] = run
            run = run + row_in[t, h, j]
        total[t, h] = run
        if t == 0 and h == 0:

            @pl.when(z < RING - 1)
            def _():
                pl.semaphore_wait(ready, RING - 1 - z)

        count = larger(t)[0]

        def send(i, _):
            send_col(t, h, count - i).start()
            return _

        lax.fori_loop(0, count, send, 0)

    def col_step(t, h):
        def add(i, beyond):
            send_col(t, h, i + 1).wait_recv()
            return beyond + col_in[t, h, i]

        beyond = lax.fori_loop(0, larger(t)[1], add, jnp.zeros((PER * part, DK), F32))
        for j in range(RING):
            row_out[t, h, j] = row_out[t, h, j] + beyond
        for d in OFFSETS:
            send_back(t, h, d).start()
        back[t, h, y] = row_out[t, h, y]

    def last_step(t, c):
        all_of(back.at[t, c], back_sem.at[t, c])
        for i in range(PER):
            h = c * PER + i
            state = back[t, c, :, pl.ds(i * part, part)].reshape(DK, DK)
            if t:
                ak[:, columns(h)] = ak[:, columns(h)] + dot(parts[1, h], right(state, 1), NT)
                av[:, columns(h)] = av[:, columns(h)] + dot(parts[0, h], right(state, 0), NN)
            else:
                aq[:, columns(h)] = aq[:, columns(h)] + dot(parts[2, h], right(state, 1), NT)

    def all_sent(order):
        for t, c in order:
            all_of(local.at[t, c], row_send.at[t, c])
            all_of(row_out.at[t, c], back_send.at[t, c])

            def sent(i, _):
                send_col(t, c, i + 1).wait_send()
                return _

            lax.fori_loop(0, larger(t)[0], sent, 0)

    def work(kinds):
        order = [(t, c) for t in kinds for c in range(chunks)]

        def load_chunk(t, c):
            for i in range(PER):
                load(2 * t, c * PER + i).start()
                load(2 * t + 1, c * PER + i).start()

        load_chunk(*order[0])
        greet_column()
        for n, (t, c) in enumerate(order):
            for i in range(PER):
                state(t, c, i)
                if n == 0 and i == 0:
                    for u, e in order[1:]:
                        load_chunk(u, e)
                    meet()
                if n == 0:
                    row_start(t, c, i, 1)
            if n > 0:
                row_start(t, c, 0, PER)
            row_in[t, c, y] = local[t, c, y]
        for h in range(heads):
            within(h)
        lag = 2
        for step in range(len(order) + lag):
            if step < len(order):
                row_step(*order[step])
            if step >= lag:
                col_step(*order[step - lag])
        for t, c in order[:-1]:
            last_step(t, c)
        all_sent(order[:-1])
        last_step(*order[-1])
        all_sent(order[-1:])

    @pl.when(z < RING // 2)
    def _():
        work((0, 1))

    @pl.when(z >= RING // 2)
    def _():
        work((1, 0))


def write_out(aq, ak, av, oq, ok, ov, sem):
    slabs = sem.shape[1]
    rows = aq.shape[0] // slabs
    copies = []
    for i, (a, o) in enumerate(((aq, oq), (ak, ok), (av, ov))):
        for j in range(slabs):
            here = pl.ds(j * rows, rows)
            copies.append(pltpu.make_async_copy(a.at[here], o.at[here], sem.at[i, j]))
    for copy in copies:
        copy.start()
    for copy in copies:
        copy.wait()


def shards(queries, keys, values, out_grad):
    length, width = queries.shape
    heads = width // DK
    part = DK // RING
    chunks = heads // PER
    held = pltpu.VMEM((length, width), F32)
    out = pltpu.HBM((length, width), F32)
    arrays = [pltpu.with_memory_space_constraint(a, pltpu.HBM) for a in (queries, keys, values, out_grad)]
    block = pltpu.VMEM((heads, length, DK), F32)
    pieces = pltpu.VMEM((2, chunks, RING, PER * part, DK), F32)
    grads = pl.pallas_call(
        functools.partial(kernel, heads),
        out_shape=(held, held, held),
        in_specs=[pl.BlockSpec(memory_space=pltpu.HBM)] * 4,
        out_specs=(pl.BlockSpec(memory_space=pltpu.VMEM),) * 3,
        scratch_shapes=[block] * 4 + [
            pltpu.VMEM((3, heads, length, 3 * DK), BF16),
            pieces,
            pieces,
            pieces,
            pltpu.VMEM((2, chunks, PER * part, DK), F32),
            pltpu.VMEM((2, chunks, RING - 1, PER * part, DK), F32),
            pieces,
            pltpu.SemaphoreType.DMA((4, heads)),
            pltpu.SemaphoreType.DMA((2, chunks)),
            pltpu.SemaphoreType.DMA((2, chunks)),
            pltpu.SemaphoreType.DMA((2, chunks, RING - 1)),
            pltpu.SemaphoreType.DMA((2, chunks, RING - 1)),
            pltpu.SemaphoreType.DMA((2, chunks)),
            pltpu.SemaphoreType.DMA((2, chunks)),
            pltpu.SemaphoreType.REGULAR,
        ],
        compiler_params=pltpu.CompilerParams(
            collective_id=0, has_side_effects=True, vmem_limit_bytes=32 * 2**20),
        cost_estimate=pl.CostEstimate(
            flops=2 * 3 * heads * length * DK * (6 * length + 5 * DK),
            bytes_accessed=7 * 4 * length * width, transcendentals=0),
        name="linear_attention_backward",
    )(*arrays)
    return pl.pallas_call(
        write_out,
        out_shape=(out, out, out),
        in_specs=[pl.BlockSpec(memory_space=pltpu.VMEM)] * 3,
        out_specs=(pl.BlockSpec(memory_space=pltpu.HBM),) * 3,
        scratch_shapes=[pltpu.SemaphoreType.DMA((3, 1))],
        name="write_out",
    )(*[pltpu.with_memory_space_constraint(a, pltpu.VMEM) for a in grads])


def solution(mesh):
    return jax.shard_map(
        shards,
        mesh=mesh,
        in_specs=(P("seq", "head"),) * 4,
        out_specs=(P("seq", "head"),) * 3,
        check_vma=False,
    )
```

```python
import functools

import jax
import jax.numpy as jnp
from jax import lax
from jax.experimental import pallas as pl
from jax.experimental.pallas import tpu as pltpu
from jax.sharding import PartitionSpec as P

DK = 128
RING = 8
MESH = pl.DeviceIdType.MESH
F32 = jnp.float32
BF16 = jnp.bfloat16
OFFSETS = (4, 3, 2, 1, 5, 6, 7)
PER = 2

NT = (((1,), (1,)), ((), ()))
NN = (((1,), (0,)), ((), ()))


def split(x):
    hi = x.astype(BF16)
    lo = (x - hi.astype(F32)).astype(BF16)
    return hi, lo


def left(x, axis):
    hi, lo = split(x)
    return jnp.concatenate([hi, lo, hi], axis=axis)


def right(x, axis):
    hi, lo = split(x)
    return jnp.concatenate([hi, hi, lo], axis=axis)


def dot(a, b, dims):
    return lax.dot_general(a, b, dims, preferred_element_type=F32)


def product(a, b, dims):
    (ca,), (cb,) = dims[0]
    return dot(left(a, ca), right(b, cb), dims)


def kernel(heads, q_hbm, k_hbm, v_hbm, g_hbm, aq, ak, av,
           q_v, k_v, v_v, g_v, parts, local, row_in, row_out, total, col_in, back,
           load_sem, row_send, row_sem, col_send, col_sem, back_send, back_sem, ready):
    me = lax.axis_index("seq")
    hd = lax.axis_index("head")
    z = lax.div(me, RING)
    y = lax.rem(me, RING)
    length = q_v.shape[1]
    part = DK // RING
    chunks = heads // PER

    def in_row(d):
        return lax.rem(y + jnp.where(lax.rem(hd, 2) == 0, d, RING - d), RING)

    def row_peer(d):
        return (z * RING + in_row(d), hd)

    def in_column(other):
        return (other * RING + y, hd)

    barrier = pltpu.get_barrier_semaphore()
    for d in OFFSETS:
        pl.semaphore_signal(barrier, inc=1, device_id=row_peer(d), device_id_type=MESH)

    def greet_column():
        def greet(d, _):
            pl.semaphore_signal(barrier, inc=1, device_id=in_column(z + d), device_id_type=MESH)
            return _

        lax.fori_loop(1, RING - z, greet, 0)

    def meet():
        pl.semaphore_wait(barrier, RING - 1 + z)

        def tell(d, _):
            pl.semaphore_signal(ready, inc=1, device_id=in_column(z - d), device_id_type=MESH)
            return _

        lax.fori_loop(1, z + 1, tell, 0)

    def columns(h):
        return pl.ds(h * DK, DK)

    def load(i, h):
        hbm, vmem = ((k_hbm, k_v), (v_hbm, v_v), (q_hbm, q_v), (g_hbm, g_v))[i]
        return pltpu.make_async_copy(hbm.at[:, columns(h)], vmem.at[h], load_sem.at[i, h])

    def send_row(t, c, d, first, count):
        some = pl.ds(first * part, count * part)
        return pltpu.make_async_remote_copy(
            src_ref=local.at[t, c, in_row(d), some], dst_ref=row_in.at[t, c, y, some],
            send_sem=row_send.at[t, c], recv_sem=row_sem.at[t, c], device_id=row_peer(d), device_id_type=MESH)

    def send_col(t, h, d):
        return pltpu.make_async_remote_copy(
            src_ref=total.at[t, h], dst_ref=col_in.at[t, h, d - 1],
            send_sem=col_send.at[t, h, d - 1], recv_sem=col_sem.at[t, h, d - 1],
            device_id=in_column(z - d if t else z + d), device_id_type=MESH)

    def send_back(t, h, d):
        return pltpu.make_async_remote_copy(
            src_ref=row_out.at[t, h, in_row(d)], dst_ref=back.at[t, h, y],
            send_sem=back_send.at[t, h], recv_sem=back_sem.at[t, h], device_id=row_peer(d), device_id_type=MESH)

    def all_of(ref, sem):
        some = ref.at[pl.ds(0, RING - 1)]
        pltpu.make_async_copy(some, some, sem).wait()

    def larger(t):
        return (z, RING - 1 - z) if t else (RING - 1 - z, z)

    def state(t, c, i):
        a, b = (q_v, g_v) if t else (k_v, v_v)
        h = c * PER + i
        load(2 * t, h).wait()
        load(2 * t + 1, h).wait()
        local[t, c, :, pl.ds(i * part, part)] = product(a[h].T, b[h], NN).reshape(RING, part, DK)

    def row_start(t, c, first, count):
        for d in OFFSETS:
            send_row(t, c, d, first, count).start()

    def within(h):
        rows = lax.broadcasted_iota(jnp.int32, (length, length), 0)
        cols = lax.broadcasted_iota(jnp.int32, (length, length), 1)
        q, k, v, g = q_v[h], k_v[h], v_v[h], g_v[h]
        k_left, v_left, g_left = left(k, 1), left(v, 1), left(g, 1)
        parts[0, h] = k_left
        parts[1, h] = v_left
        parts[2, h] = g_left
        scores_t = jnp.where(rows <= cols, dot(k_left, right(q, 1), NT), 0.0)
        av[:, columns(h)] = product(scores_t, g, NN)
        dscores = jnp.where(rows >= cols, dot(g_left, right(v, 1), NT), 0.0)
        aq[:, columns(h)] = product(dscores, k, NN)
        dscores_t = jnp.where(rows <= cols, dot(v_left, right(g, 1), NT), 0.0)
        ak[:, columns(h)] = product(dscores_t, q, NN)

    def row_step(t, h):
        all_of(row_in.at[t, h], row_sem.at[t, h])
        run = jnp.zeros((PER * part, DK), F32)
        for j in (reversed(range(RING)) if t else range(RING)):
            row_out[t, h, j] = run
            run = run + row_in[t, h, j]
        total[t, h] = run
        if t == 0 and h == 0:

            @pl.when(z < RING - 1)
            def _():
                pl.semaphore_wait(ready, RING - 1 - z)

        count = larger(t)[0]

        def send(i, _):
            send_col(t, h, count - i).start()
            return _

        lax.fori_loop(0, count, send, 0)

    def col_step(t, h):
        def add(i, beyond):
            send_col(t, h, i + 1).wait_recv()
            return beyond + col_in[t, h, i]

        beyond = lax.fori_loop(0, larger(t)[1], add, jnp.zeros((PER * part, DK), F32))
        for j in range(RING):
            row_out[t, h, j] = row_out[t, h, j] + beyond
        for d in OFFSETS:
            send_back(t, h, d).start()
        back[t, h, y] = row_out[t, h, y]

    def last_step(t, c):
        all_of(back.at[t, c], back_sem.at[t, c])
        for i in range(PER):
            h = c * PER + i
            state = back[t, c, :, pl.ds(i * part, part)].reshape(DK, DK)
            if t:
                ak[:, columns(h)] = ak[:, columns(h)] + dot(parts[1, h], right(state, 1), NT)
                av[:, columns(h)] = av[:, columns(h)] + dot(parts[0, h], right(state, 0), NN)
            else:
                aq[:, columns(h)] = aq[:, columns(h)] + dot(parts[2, h], right(state, 1), NT)

    def all_sent(order):
        for t, c in order:
            all_of(local.at[t, c], row_send.at[t, c])
            all_of(row_out.at[t, c], back_send.at[t, c])

            def sent(i, _):
                send_col(t, c, i + 1).wait_send()
                return _

            lax.fori_loop(0, larger(t)[0], sent, 0)

    def work(kinds):
        order = [(t, c) for t in kinds for c in range(chunks)]

        def load_chunk(t, c):
            for i in range(PER):
                load(2 * t, c * PER + i).start()
                load(2 * t + 1, c * PER + i).start()

        load_chunk(*order[0])
        greet_column()
        for n, (t, c) in enumerate(order):
            for i in range(PER):
                state(t, c, i)
                if n == 0 and i == 0:
                    for u, e in order[1:]:
                        load_chunk(u, e)
                    meet()
                if n == 0:
                    row_start(t, c, i, 1)
            if n > 0:
                row_start(t, c, 0, PER)
            row_in[t, c, y] = local[t, c, y]
        core = lax.rem(hd, 2)
        early = heads // 2
        for h in range(early):
            within(h)

        @pl.when(core == 1)
        def _():
            for h in range(early, heads):
                within(h)

        lag = 2
        for step in range(len(order) + lag):
            if step < len(order):
                row_step(*order[step])
            if step >= lag:
                col_step(*order[step - lag])
            if step == 0:
                @pl.when(core == 0)
                def _():
                    for h in range(early, heads):
                        within(h)

        for t, c in order[:-1]:
            last_step(t, c)
        all_sent(order[:-1])
        last_step(*order[-1])
        all_sent(order[-1:])

    @pl.when(z < RING // 2)
    def _():
        work((0, 1))

    @pl.when(z >= RING // 2)
    def _():
        work((1, 0))


def write_out(aq, ak, av, oq, ok, ov, sem):
    slabs = sem.shape[1]
    rows = aq.shape[0] // slabs
    copies = []
    for i, (a, o) in enumerate(((aq, oq), (ak, ok), (av, ov))):
        for j in range(slabs):
            here = pl.ds(j * rows, rows)
            copies.append(pltpu.make_async_copy(a.at[here], o.at[here], sem.at[i, j]))
    for copy in copies:
        copy.start()
    for copy in copies:
        copy.wait()


def shards(queries, keys, values, out_grad):
    length, width = queries.shape
    heads = width // DK
    part = DK // RING
    chunks = heads // PER
    held = pltpu.VMEM((length, width), F32)
    out = pltpu.HBM((length, width), F32)
    arrays = [pltpu.with_memory_space_constraint(a, pltpu.HBM) for a in (queries, keys, values, out_grad)]
    block = pltpu.VMEM((heads, length, DK), F32)
    pieces = pltpu.VMEM((2, chunks, RING, PER * part, DK), F32)
    grads = pl.pallas_call(
        functools.partial(kernel, heads),
        out_shape=(held, held, held),
        in_specs=[pl.BlockSpec(memory_space=pltpu.HBM)] * 4,
        out_specs=(pl.BlockSpec(memory_space=pltpu.VMEM),) * 3,
        scratch_shapes=[block] * 4 + [
            pltpu.VMEM((3, heads, length, 3 * DK), BF16),
            pieces,
            pieces,
            pieces,
            pltpu.VMEM((2, chunks, PER * part, DK), F32),
            pltpu.VMEM((2, chunks, RING - 1, PER * part, DK), F32),
            pieces,
            pltpu.SemaphoreType.DMA((4, heads)),
            pltpu.SemaphoreType.DMA((2, chunks)),
            pltpu.SemaphoreType.DMA((2, chunks)),
            pltpu.SemaphoreType.DMA((2, chunks, RING - 1)),
            pltpu.SemaphoreType.DMA((2, chunks, RING - 1)),
            pltpu.SemaphoreType.DMA((2, chunks)),
            pltpu.SemaphoreType.DMA((2, chunks)),
            pltpu.SemaphoreType.REGULAR,
        ],
        compiler_params=pltpu.CompilerParams(
            collective_id=0, has_side_effects=True, vmem_limit_bytes=32 * 2**20),
        cost_estimate=pl.CostEstimate(
            flops=2 * 3 * heads * length * DK * (6 * length + 5 * DK),
            bytes_accessed=7 * 4 * length * width, transcendentals=0),
        name="linear_attention_backward",
    )(*arrays)
    return pl.pallas_call(
        write_out,
        out_shape=(out, out, out),
        in_specs=[pl.BlockSpec(memory_space=pltpu.VMEM)] * 3,
        out_specs=(pl.BlockSpec(memory_space=pltpu.HBM),) * 3,
        scratch_shapes=[pltpu.SemaphoreType.DMA((3, 1))],
        name="write_out",
    )(*[pltpu.with_memory_space_constraint(a, pltpu.VMEM) for a in grads])


def solution(mesh):
    return jax.shard_map(
        shards,
        mesh=mesh,
        in_specs=(P("seq", "head"),) * 4,
        out_specs=(P("seq", "head"),) * 3,
        check_vma=False,
    )
```

```python
import functools

import jax
import jax.numpy as jnp
from jax import lax
from jax.experimental import pallas as pl
from jax.experimental.pallas import tpu as pltpu
from jax.sharding import PartitionSpec as P

DK = 128
RING = 8
MESH = pl.DeviceIdType.MESH
F32 = jnp.float32
BF16 = jnp.bfloat16
OFFSETS = (4, 3, 2, 1, 5, 6, 7)
PER = 2

NT = (((1,), (1,)), ((), ()))
NN = (((1,), (0,)), ((), ()))


def split(x):
    hi = x.astype(BF16)
    lo = (x - hi.astype(F32)).astype(BF16)
    return hi, lo


def left(x, axis):
    hi, lo = split(x)
    return jnp.concatenate([hi, lo, hi], axis=axis)


def right(x, axis):
    hi, lo = split(x)
    return jnp.concatenate([hi, hi, lo], axis=axis)


def dot(a, b, dims):
    return lax.dot_general(a, b, dims, preferred_element_type=F32)


def product(a, b, dims):
    (ca,), (cb,) = dims[0]
    return dot(left(a, ca), right(b, cb), dims)


def kernel(heads, q_hbm, k_hbm, v_hbm, g_hbm, aq, ak, av,
           q_v, k_v, v_v, g_v, parts, local, row_in, row_out, total, col_in, back,
           load_sem, row_send, row_sem, col_send, col_sem, back_send, back_sem, ready):
    me = lax.axis_index("seq")
    hd = lax.axis_index("head")
    z = lax.div(me, RING)
    y = lax.rem(me, RING)
    length = q_v.shape[1]
    part = DK // RING
    chunks = heads // PER

    def in_row(d):
        return lax.rem(y + jnp.where(lax.rem(hd, 2) == 0, d, RING - d), RING)

    def row_peer(d):
        return (z * RING + in_row(d), hd)

    def in_column(other):
        return (other * RING + y, hd)

    barrier = pltpu.get_barrier_semaphore()
    for d in OFFSETS:
        pl.semaphore_signal(barrier, inc=1, device_id=row_peer(d), device_id_type=MESH)

    def greet_column():
        def greet(d, _):
            pl.semaphore_signal(barrier, inc=1, device_id=in_column(z + d), device_id_type=MESH)
            return _

        lax.fori_loop(1, RING - z, greet, 0)

    def meet():
        pl.semaphore_wait(barrier, RING - 1 + z)

    def tell_column():
        def tell(d, _):
            pl.semaphore_signal(ready, inc=1, device_id=in_column(z - d), device_id_type=MESH)
            return _

        lax.fori_loop(1, z + 1, tell, 0)

    def columns(h):
        return pl.ds(h * DK, DK)

    def load(i, h):
        hbm, vmem = ((k_hbm, k_v), (v_hbm, v_v), (q_hbm, q_v), (g_hbm, g_v))[i]
        return pltpu.make_async_copy(hbm.at[:, columns(h)], vmem.at[h], load_sem.at[i, h])

    def send_row(t, c, d, first, count):
        some = pl.ds(first * part, count * part)
        return pltpu.make_async_remote_copy(
            src_ref=local.at[t, c, in_row(d), some], dst_ref=row_in.at[t, c, y, some],
            send_sem=row_send.at[t, c], recv_sem=row_sem.at[t, c], device_id=row_peer(d), device_id_type=MESH)

    def send_col(t, h, d):
        return pltpu.make_async_remote_copy(
            src_ref=total.at[t, h], dst_ref=col_in.at[t, h, d - 1],
            send_sem=col_send.at[t, h, d - 1], recv_sem=col_sem.at[t, h, d - 1],
            device_id=in_column(z - d if t else z + d), device_id_type=MESH)

    def send_back(t, h, d):
        return pltpu.make_async_remote_copy(
            src_ref=row_out.at[t, h, in_row(d)], dst_ref=back.at[t, h, y],
            send_sem=back_send.at[t, h], recv_sem=back_sem.at[t, h], device_id=row_peer(d), device_id_type=MESH)

    def all_of(ref, sem):
        some = ref.at[pl.ds(0, RING - 1)]
        pltpu.make_async_copy(some, some, sem).wait()

    def larger(t):
        return (z, RING - 1 - z) if t else (RING - 1 - z, z)

    def state(t, c, i):
        a, b = (q_v, g_v) if t else (k_v, v_v)
        h = c * PER + i
        load(2 * t, h).wait()
        load(2 * t + 1, h).wait()
        local[t, c, :, pl.ds(i * part, part)] = product(a[h].T, b[h], NN).reshape(RING, part, DK)

    def row_start(t, c, first, count):
        for d in OFFSETS:
            send_row(t, c, d, first, count).start()

    def within(h):
        rows = lax.broadcasted_iota(jnp.int32, (length, length), 0)
        cols = lax.broadcasted_iota(jnp.int32, (length, length), 1)
        q, k, v, g = q_v[h], k_v[h], v_v[h], g_v[h]
        k_left, v_left, g_left = left(k, 1), left(v, 1), left(g, 1)
        parts[0, h] = k_left
        parts[1, h] = v_left
        parts[2, h] = g_left
        scores_t = jnp.where(rows <= cols, dot(k_left, right(q, 1), NT), 0.0)
        av[:, columns(h)] = product(scores_t, g, NN)
        dscores = jnp.where(rows >= cols, dot(g_left, right(v, 1), NT), 0.0)
        aq[:, columns(h)] = product(dscores, k, NN)
        dscores_t = jnp.where(rows <= cols, dot(v_left, right(g, 1), NT), 0.0)
        ak[:, columns(h)] = product(dscores_t, q, NN)

    def row_step(t, h):
        all_of(row_in.at[t, h], row_sem.at[t, h])
        run = jnp.zeros((PER * part, DK), F32)
        for j in (reversed(range(RING)) if t else range(RING)):
            row_out[t, h, j] = run
            run = run + row_in[t, h, j]
        total[t, h] = run
        if t == 0 and h == 0:

            @pl.when(z < RING - 1)
            def _():
                pl.semaphore_wait(ready, RING - 1 - z)

        count = larger(t)[0]

        def send(i, _):
            send_col(t, h, count - i).start()
            return _

        lax.fori_loop(0, count, send, 0)

    def col_step(t, h):
        def add(i, beyond):
            send_col(t, h, i + 1).wait_recv()
            return beyond + col_in[t, h, i]

        beyond = lax.fori_loop(0, larger(t)[1], add, jnp.zeros((PER * part, DK), F32))
        for j in range(RING):
            row_out[t, h, j] = row_out[t, h, j] + beyond
        for d in OFFSETS:
            send_back(t, h, d).start()
        back[t, h, y] = row_out[t, h, y]

    def last_step(t, c):
        all_of(back.at[t, c], back_sem.at[t, c])
        for i in range(PER):
            h = c * PER + i
            state = back[t, c, :, pl.ds(i * part, part)].reshape(DK, DK)
            if t:
                ak[:, columns(h)] = ak[:, columns(h)] + dot(parts[1, h], right(state, 1), NT)
                av[:, columns(h)] = av[:, columns(h)] + dot(parts[0, h], right(state, 0), NN)
            else:
                aq[:, columns(h)] = aq[:, columns(h)] + dot(parts[2, h], right(state, 1), NT)

    def all_sent(order):
        for t, c in order:
            all_of(local.at[t, c], row_send.at[t, c])
            all_of(row_out.at[t, c], back_send.at[t, c])

            def sent(i, _):
                send_col(t, c, i + 1).wait_send()
                return _

            lax.fori_loop(0, larger(t)[0], sent, 0)

    def work(kinds):
        order = [(t, c) for t in kinds for c in range(chunks)]

        def load_chunk(t, c):
            for i in range(PER):
                load(2 * t, c * PER + i).start()
                load(2 * t + 1, c * PER + i).start()

        load_chunk(*order[0])
        greet_column()
        for n, (t, c) in enumerate(order):
            for i in range(PER):
                state(t, c, i)
                if n == 0 and i == 0:
                    meet()
                if n == 0:
                    row_start(t, c, i, 1)
                if n == 0 and i == 0:
                    for u, e in order[1:]:
                        load_chunk(u, e)
                    tell_column()
            if n > 0:
                row_start(t, c, 0, PER)
            row_in[t, c, y] = local[t, c, y]
        for h in range(heads):
            within(h)
        lag = 2
        for step in range(len(order) + lag):
            if step < len(order):
                row_step(*order[step])
            if step >= lag:
                col_step(*order[step - lag])
        for t, c in order[:-1]:
            last_step(t, c)
        all_sent(order[:-1])
        last_step(*order[-1])
        all_sent(order[-1:])

    @pl.when(z < RING // 2)
    def _():
        work((0, 1))

    @pl.when(z >= RING // 2)
    def _():
        work((1, 0))


def write_out(aq, ak, av, oq, ok, ov, sem):
    slabs = sem.shape[1]
    rows = aq.shape[0] // slabs
    copies = []
    for i, (a, o) in enumerate(((aq, oq), (ak, ok), (av, ov))):
        for j in range(slabs):
            here = pl.ds(j * rows, rows)
            copies.append(pltpu.make_async_copy(a.at[here], o.at[here], sem.at[i, j]))
    for copy in copies:
        copy.start()
    for copy in copies:
        copy.wait()


def shards(queries, keys, values, out_grad):
    length, width = queries.shape
    heads = width // DK
    part = DK // RING
    chunks = heads // PER
    held = pltpu.VMEM((length, width), F32)
    out = pltpu.HBM((length, width), F32)
    arrays = [pltpu.with_memory_space_constraint(a, pltpu.HBM) for a in (queries, keys, values, out_grad)]
    block = pltpu.VMEM((heads, length, DK), F32)
    pieces = pltpu.VMEM((2, chunks, RING, PER * part, DK), F32)
    grads = pl.pallas_call(
        functools.partial(kernel, heads),
        out_shape=(held, held, held),
        in_specs=[pl.BlockSpec(memory_space=pltpu.HBM)] * 4,
        out_specs=(pl.BlockSpec(memory_space=pltpu.VMEM),) * 3,
        scratch_shapes=[block] * 4 + [
            pltpu.VMEM((3, heads, length, 3 * DK), BF16),
            pieces,
            pieces,
            pieces,
            pltpu.VMEM((2, chunks, PER * part, DK), F32),
            pltpu.VMEM((2, chunks, RING - 1, PER * part, DK), F32),
            pieces,
            pltpu.SemaphoreType.DMA((4, heads)),
            pltpu.SemaphoreType.DMA((2, chunks)),
            pltpu.SemaphoreType.DMA((2, chunks)),
            pltpu.SemaphoreType.DMA((2, chunks, RING - 1)),
            pltpu.SemaphoreType.DMA((2, chunks, RING - 1)),
            pltpu.SemaphoreType.DMA((2, chunks)),
            pltpu.SemaphoreType.DMA((2, chunks)),
            pltpu.SemaphoreType.REGULAR,
        ],
        compiler_params=pltpu.CompilerParams(
            collective_id=0, has_side_effects=True, vmem_limit_bytes=32 * 2**20),
        cost_estimate=pl.CostEstimate(
            flops=2 * 3 * heads * length * DK * (6 * length + 5 * DK),
            bytes_accessed=7 * 4 * length * width, transcendentals=0),
        name="linear_attention_backward",
    )(*arrays)
    return pl.pallas_call(
        write_out,
        out_shape=(out, out, out),
        in_specs=[pl.BlockSpec(memory_space=pltpu.VMEM)] * 3,
        out_specs=(pl.BlockSpec(memory_space=pltpu.HBM),) * 3,
        scratch_shapes=[pltpu.SemaphoreType.DMA((3, 1))],
        name="write_out",
    )(*[pltpu.with_memory_space_constraint(a, pltpu.VMEM) for a in grads])


def solution(mesh):
    return jax.shard_map(
        shards,
        mesh=mesh,
        in_specs=(P("seq", "head"),) * 4,
        out_specs=(P("seq", "head"),) * 3,
        check_vma=False,
    )
```
